32 devices in a mesh: groups: 2 (over y), dp: 4 (over z), tensor: 4 (over x, core).
Axes of the slice: x: 2, y: 2, z: 4, core: 2. Of those that a mesh axis runs over, the one named last changes fastest.
Arguments:
- queries: bfloat16 [128, 64, 12288], P(('groups', 'dp'), None, 'tensor'), parts along dimension 0, may hold values from -360 to 360
- new_keys: bfloat16 [128, 64, 1024], P(('groups', 'dp'), None, 'tensor'), parts along dimension 0, may hold values from -6 to 6
- new_values: bfloat16 [128, 64, 1024], P(('groups', 'dp'), None, 'tensor'), parts along dimension 0, may hold values from -6 to 6
- key_down: bfloat16 [1024, 384], P('tensor'), may hold values from -0.1875 to 0.1875
- key_up: bfloat16 [384, 1024], P(None, 'tensor'), may hold values from -0.3125 to 0.3125
- cache_latent: bfloat16 [128, 1024, 384], P(('groups', 'dp'), 'tensor'), parts along dimension 0, may hold values from -6 to 6
- cache_values: bfloat16 [128, 1024, 1024], P(('groups', 'dp'), None, 'tensor'), parts along dimension 0, may hold values from -6 to 6
- cache_lengths: int32 [128], P('groups'), parts along dimension 0, may hold values from 1 to 1024, as said below
- task_source: int32 [128], P('groups'), parts along dimension 0, may hold values from 0 to 63, as said below
Outputs:
- attended: bfloat16 [128, 64, 12288], P(('groups', 'dp'), None, 'tensor'), parts along dimension 0
- new_latent: bfloat16 [128, 64, 384], P(('groups', 'dp'), 'tensor'), parts along dimension 0
The draws below stay inside these ranges and needn't reach their ends.
There are 2 independent parts, one for each index of `groups`. The reference program is written for one: setup_inputs(seed, part) draws one part's arguments, and reference() takes and returns one part's arrays. A program takes and returns all parts, laid end to end along the dimension named above; an argument that names none is the same for every part. Nothing has to cross between parts.
Inputs may be any that keep to these rules, and one draw needn't show every extreme that they name: `cache_lengths`: request g is request g % 16 of dp index g // 16, which holds its cache rows; within one part a request with all 1024 positions exists, and the positions at or after a request's length hold no meaning. `task_source`: task t is run by dp index t // 16. Every request is extended by exactly one task. Among the tasks of one dp index, at most 4 extend requests held by one same dp index, and some index pairs have exactly 4. For each slot s of 16, the distance (runner minus holder, modulo 4) of task slot s is the same on every dp index.
All inputs are finite; a program needn't handle non-finite values.
Results may differ from the reference program's by a relative error of at most 0.0025.
The reference program's roundings to bfloat16 on the way count: a program that leaves them out, or rounds other values in their place, can miss the bound.
Values may be sent and summed in bfloat16 or wider, within the bound.
A program may use at most 192 MiB of HBM per device.

```python
import jax
import jax.numpy as jnp
from jax import lax

HQ = 96
HK = 8
HD = 128
RANK = 384
CH = 64
REQ_DEV = 16
MAXLEN = 1024
OWNERS = 4
MOST = 4
TASKS = 64


def draw_queries(key, part):
    key = jax.random.fold_in(key, 7)
    base_key = jax.random.fold_in(key, 0)
    values = jnp.clip(jax.random.normal(base_key, (TASKS, CH, HQ * HD), jnp.float32), -6.0, 6.0)
    return values.astype(jnp.bfloat16)


def draw_cache_lengths(key, part):
    key = jax.random.fold_in(key, 5)
    level_key, heavy_key, length_key = jax.random.split(key, 3)
    level = jax.random.randint(level_key, (OWNERS, 1), 1, 9)
    heavy = jax.random.randint(heavy_key, (), 0, OWNERS)
    is_heavy = jnp.arange(OWNERS)[:, None] == heavy
    level = jnp.where(is_heavy, 8, level)
    ceiling = level * MAXLEN // 8
    noise = jax.random.randint(length_key, (OWNERS, REQ_DEV), 0, 1 << 20)
    lengths = 1 + noise % ceiling
    lengths = jnp.where(is_heavy, MAXLEN, lengths)
    return lengths.reshape(TASKS).astype(jnp.int32)


def draw_task_source(key, part):
    key = jax.random.fold_in(key, 11)
    pick_key, shuffle_key, order_key = jax.random.split(key, 3)
    picks = jax.random.permutation(pick_key, OWNERS)[:REQ_DEV // MOST]
    shifts = jax.random.permutation(shuffle_key, jnp.repeat(picks, MOST))
    orders = jax.vmap(lambda sub: jax.random.permutation(sub, REQ_DEV))(jax.random.split(order_key, OWNERS))
    runner = jnp.arange(OWNERS)[:, None]
    holder = (runner - shifts[None, :]) % OWNERS
    request = orders[holder, jnp.arange(REQ_DEV)[None, :]]
    return (holder * REQ_DEV + request).reshape(TASKS).astype(jnp.int32)


def level_of(stream_key, shape, cuts, smallest, high):
    level, own = 1.0, jax.random.fold_in(stream_key, 6)
    for dim, blocks in cuts:
        heights = jnp.exp(jax.random.uniform(jax.random.fold_in(own, dim), (blocks,), jnp.float32, smallest / len(cuts), high / len(cuts)))
        level = level * jnp.repeat(heights, shape[dim] // blocks).reshape([-1 if axis == dim else 1 for axis in range(len(shape))])
    return level


def centred(own_key, dims, deviation, most, cuts=(), held_as=jnp.bfloat16):
    entries = jax.random.normal(own_key, dims, jnp.float32) * deviation
    if len(cuts) > 0:
        entries = level_of(own_key, dims, cuts, -0.22, 0.18) * entries
    return jnp.clip(entries, min=-most, max=most).astype(held_as)


def setup_inputs(seed: int = 0, part: int = 0) -> dict:
    key_of = jax.random.split(jax.random.key(seed), 10)
    own_keys = jax.random.split(jax.random.fold_in(key_of[9], part), 10)
    queries = draw_queries(jax.random.fold_in(jax.random.fold_in(key_of[9], part), 71), part)
    new_keys = centred(own_keys[1], (TASKS, CH, HK * HD), 1.0, 6.0, ((0, 4), (2, 4)))
    new_values = centred(own_keys[2], (TASKS, CH, HK * HD), 1.0, 6.0, ((0, 4), (2, 4)))
    key_down = centred(key_of[3], (HK * HD, RANK), (HK * HD) ** -0.5, 0.1875, ((0, 4),))
    key_up = centred(key_of[4], (RANK, HK * HD), RANK ** -0.5, 0.3125, ((1, 4),))
    cache_latent = centred(own_keys[5], (TASKS, MAXLEN, RANK), 1.0, 6.0, ((0, 4), (1, 4)))
    cache_values = centred(own_keys[6], (TASKS, MAXLEN, HK * HD), 1.0, 6.0, ((0, 4), (2, 4)))
    cache_lengths = draw_cache_lengths(jax.random.fold_in(jax.random.fold_in(key_of[9], part), 71), part)
    task_source = draw_task_source(jax.random.fold_in(jax.random.fold_in(key_of[9], part), 71), part)
    return dict(queries=queries, new_keys=new_keys, new_values=new_values, key_down=key_down, key_up=key_up, cache_latent=cache_latent, cache_values=cache_values, cache_lengths=cache_lengths, task_source=task_source)


def rounded(values):
    return lax.optimization_barrier(values.astype(jnp.bfloat16)).astype(jnp.float32)


def reference(queries, new_keys, new_values, key_down, key_up, cache_latent, cache_values, cache_lengths, task_source):
    per_kv = HQ // HK
    score_scale = HD ** -0.5
    latent_new = jnp.einsum('tck,kl->tcl', new_keys.astype(jnp.float32), key_down.astype(jnp.float32)).astype(jnp.bfloat16)
    keys_new = jnp.einsum('tcl,lk->tck', latent_new.astype(jnp.float32), key_up.astype(jnp.float32)).astype(jnp.bfloat16)
    causal = jnp.arange(CH)[:, None] >= jnp.arange(CH)[None, :]
    positions = jnp.arange(MAXLEN)

    def one_task(task):
        request = task_source[task]
        length = cache_lengths[request]
        query_heads = queries[task].astype(jnp.float32).reshape(CH, HK, per_kv, HD)
        cache_keys = rounded(jnp.dot(cache_latent[request], key_up, preferred_element_type=jnp.float32)).reshape(MAXLEN, HK, HD)
        cache_vals = cache_values[request].astype(jnp.float32).reshape(MAXLEN, HK, HD)
        scores = jnp.einsum('chgd,jhd->hgcj', query_heads, cache_keys) * score_scale
        scores = jnp.where(positions < length, scores, -1e30)
        prefix_max = jnp.max(scores, axis=-1, keepdims=True)
        powers = jnp.exp(scores - prefix_max)
        prefix_total = jnp.sum(powers, axis=-1, keepdims=True)
        prefix_out = rounded(jnp.einsum('hgcj,jhd->hgcd', rounded(powers), cache_vals) / prefix_total)
        log_total = prefix_max + jnp.log(prefix_total)
        new_heads = keys_new[task].astype(jnp.float32).reshape(CH, HK, HD)
        new_vals = new_values[task].astype(jnp.float32).reshape(CH, HK, HD)
        own_scores = jnp.einsum('chgd,jhd->hgcj', query_heads, new_heads) * score_scale
        own_scores = jnp.where(causal, own_scores, -1e30)
        own_max = jnp.max(own_scores, axis=-1, keepdims=True)
        own_powers = jnp.exp(own_scores - own_max)
        own_total = jnp.sum(own_powers, axis=-1, keepdims=True)
        own_sum = jnp.einsum('hgcj,jhd->hgcd', rounded(own_powers), new_vals)
        top = jnp.maximum(log_total, own_max)
        prefix_weight = jnp.exp(log_total - top)
        own_weight = jnp.exp(own_max - top)
        merged = (prefix_weight * prefix_out + own_weight * own_sum) / (prefix_weight + own_weight * own_total)
        return jnp.transpose(merged, (2, 0, 1, 3)).reshape(CH, HQ * HD).astype(jnp.bfloat16)

    attended = lax.map(one_task, jnp.arange(TASKS))
    return attended, latent_new
```

```python
import functools
import math

import jax
import jax.numpy as jnp
from jax import lax
from jax.experimental import pallas as pl
from jax.experimental.pallas import tpu as pltpu
from jax.sharding import PartitionSpec as P

HD = 128
SCALE = HD ** (-0.5)
POWER = SCALE * math.log2(math.e)
LOW = -1e30


def attend_kernel(
    slot_ref,
    latent_place_ref,
    value_place_ref,
    length_ref,
    query_ref,
    latent_ref,
    value_ref,
    up_ref,
    own_latent_ref,
    own_value_ref,
    *rest,
):
    out_ref, rows_ref, keys_ref = rest[-3:]
    new_rows = query_ref.shape[1]
    per_kv = query_ref.shape[2] // HD
    parts, _, part_rows, _ = latent_ref.shape
    longest = parts * part_rows
    step = math.gcd(longest, 256)
    all_rows = per_kv * new_rows
    block = math.gcd(all_rows, 256)
    length = length_ref[pl.program_id(0)]
    up = up_ref[...]
    for g in range(per_kv):
        rows_ref[g * new_rows : (g + 1) * new_rows, :] = query_ref[0, :, g * HD : (g + 1) * HD]
    own_keys = jnp.dot(own_latent_ref[0], up, preferred_element_type=jnp.float32).astype(
        jnp.bfloat16
    )

    def attend(width):
        for p in range(width // part_rows):
            keys_ref[p * part_rows : (p + 1) * part_rows, :] = jnp.dot(
                latent_ref[p, 0], up, preferred_element_type=jnp.float32
            ).astype(jnp.bfloat16)
        for b in range(all_rows // block):
            rows = rows_ref[b * block : (b + 1) * block, :]
            scores = lax.dot_general(
                rows,
                keys_ref[0:width, :],
                (((1,), (1,)), ((), ())),
                preferred_element_type=jnp.float32,
            )
            first = width - step
            position = first + lax.broadcasted_iota(jnp.int32, (block, step), 1)
            last = jnp.where(position < length, scores[:, first:], LOW)
            scores = last if first == 0 else jnp.concatenate([scores[:, :first], last], axis=1)
            top_score = jnp.max(scores, axis=-1, keepdims=True)
            powers = jnp.exp2((scores - top_score) * POWER)
            total = jnp.sum(powers, axis=-1, keepdims=True)
            prefix = jnp.dot(
                powers.astype(jnp.bfloat16),
                value_ref[0, 0:width, :],
                preferred_element_type=jnp.float32,
            )
            prefix = (prefix / total).astype(jnp.bfloat16).astype(jnp.float32)
            log_total = top_score * SCALE + jnp.log(total)
            own = (
                lax.dot_general(
                    rows, own_keys, (((1,), (1,)), ((), ())), preferred_element_type=jnp.float32
                )
                * SCALE
            )
            row = lax.broadcasted_iota(jnp.int32, own.shape, 0) % new_rows
            own = jnp.where(row >= lax.broadcasted_iota(jnp.int32, own.shape, 1), own, LOW)
            own_max = jnp.max(own, axis=-1, keepdims=True)
            own_powers = jnp.exp(own - own_max)
            own_total = jnp.sum(own_powers, axis=-1, keepdims=True)
            own_sum = jnp.dot(
                own_powers.astype(jnp.bfloat16),
                own_value_ref[0],
                preferred_element_type=jnp.float32,
            )
            top = jnp.maximum(log_total, own_max)
            prefix_weight = jnp.exp(log_total - top)
            own_weight = jnp.exp(own_max - top)
            merged = (prefix_weight * prefix + own_weight * own_sum) / (
                prefix_weight + own_weight * own_total
            )
            merged = merged.astype(jnp.bfloat16)
            for i in range(block // new_rows):
                g = b * (block // new_rows) + i
                out_ref[0, :, g * HD : (g + 1) * HD] = merged[i * new_rows : (i + 1) * new_rows]

    for width in range(step, longest + 1, step):
        pl.when((length > width - step) & (length <= width))(functools.partial(attend, width))


def attend(
    slots,
    latent_places,
    value_places,
    lengths,
    queries,
    latents,
    values,
    key_up,
    own_latent,
    own_values,
    before,
):
    tasks = slots.shape[0]
    _, new_rows, qwidth = queries.shape
    parts, _, part_rows, rank = latents.shape
    longest, kwidth = values.shape[1:]
    kv_heads = kwidth // HD
    width = qwidth // kv_heads
    in_specs = [
        pl.BlockSpec((1, new_rows, width), lambda t, h, s, p, v, n: (s[t], 0, h)),
        pl.BlockSpec((parts, 1, part_rows, rank), lambda t, h, s, p, v, n: (0, p[t], 0, 0)),
        pl.BlockSpec((1, longest, HD), lambda t, h, s, p, v, n: (v[t], 0, h)),
        pl.BlockSpec((rank, HD), lambda t, h, s, p, v, n: (0, h)),
        pl.BlockSpec((1, new_rows, rank), lambda t, h, s, p, v, n: (s[t], 0, 0)),
        pl.BlockSpec((1, new_rows, HD), lambda t, h, s, p, v, n: (s[t], 0, h)),
    ]
    operands = [
        slots,
        latent_places,
        value_places,
        lengths,
        queries,
        latents,
        values,
        key_up,
        own_latent,
        own_values,
    ]
    aliases = {}
    if before is not None:
        in_specs.append(pl.BlockSpec(memory_space=pl.ANY))
        aliases = {len(operands): 0}
        operands.append(before)
    rows = width // HD * new_rows
    return pl.pallas_call(
        attend_kernel,
        grid_spec=pltpu.PrefetchScalarGridSpec(
            num_scalar_prefetch=4,
            grid=(tasks, kv_heads),
            in_specs=in_specs,
            out_specs=pl.BlockSpec((1, new_rows, width), lambda t, h, s, p, v, n: (s[t], 0, h)),
            scratch_shapes=[
                pltpu.VMEM((rows, HD), jnp.bfloat16),
                pltpu.VMEM((longest, HD), jnp.bfloat16),
            ],
        ),
        out_shape=jax.ShapeDtypeStruct(queries.shape, queries.dtype),
        input_output_aliases=aliases,
        compiler_params=pltpu.CompilerParams(vmem_limit_bytes=40 * 1024 * 1024),
        cost_estimate=pl.CostEstimate(
            flops=tasks * kv_heads * rows * longest * HD * 8,
            bytes_accessed=tasks * (2 * new_rows * qwidth + longest * (kwidth + rank)) * 2,
            transcendentals=tasks * kv_heads * rows * longest,
        ),
    )(*operands)


def on_device(
    queries,
    new_keys,
    new_values,
    key_down,
    key_up,
    cache_latent,
    cache_values,
    cache_lengths,
    task_source,
):
    task_count, new_rows, _ = queries.shape
    owners = lax.axis_size("dp")
    me = lax.axis_index("dp")
    depth = max(2, task_count // owners)
    share_rows = new_rows // lax.axis_size("tensor")

    source = task_source.reshape(owners, task_count)
    request = source % task_count
    distance = (owners - source[0] // task_count) % owners
    same = distance[:, None] == distance[None, :]
    earlier = jnp.arange(task_count)[None, :] < jnp.arange(task_count)[:, None]
    place = distance * depth + jnp.sum(same & earlier, axis=1)
    places = jnp.arange(owners * depth)
    slot_at = jnp.sum(
        jnp.where(place[None, :] == places[:, None], jnp.arange(task_count)[None, :], 0), axis=1
    ).astype(jnp.int32)
    my_source = lax.dynamic_index_in_dim(source, me, 0, keepdims=False)
    my_lengths = jnp.take(cache_lengths, my_source, mode="clip")

    def picked(shift):
        wanted = lax.dynamic_index_in_dim(request, (me + shift) % owners, 0, keepdims=False)
        return jnp.take(wanted, slot_at[shift * depth : (shift + 1) * depth], mode="clip")

    in_flight = []

    def send(array, shift):
        if len(in_flight) >= 2:
            array, in_flight[-2] = lax.optimization_barrier((array, in_flight[-2]))
        pairs = [(i, (i + shift) % owners) for i in range(owners)]
        in_flight.append(lax.ppermute(array, "dp", pairs))
        return len(in_flight) - 1

    shifts = sorted(range(1, owners), key=lambda d: (min(d, owners - d), d))
    requests = [picked(d) for d in range(owners)]
    latent_at = {d: send(jnp.take(cache_latent, requests[d], axis=0, mode="clip"), d) for d in shifts}
    value_at = {}
    for d in shifts:
        pieces = 2 if d == shifts[-1] and depth % 2 == 0 else 1
        for i in range(pieces):
            part = requests[d][i * depth // pieces : (i + 1) * depth // pieces]
            value_at[d, i] = send(jnp.take(cache_values, part, axis=0, mode="clip"), d)

    all_keys = lax.all_gather(new_keys, "tensor")
    all_down = lax.all_gather(key_down, "tensor")
    own_latent = jnp.einsum(
        "trck,tkl->rcl", all_keys, all_down, preferred_element_type=jnp.float32
    ).astype(jnp.bfloat16)
    latent_out = lax.dynamic_slice_in_dim(
        own_latent, lax.axis_index("tensor") * share_rows, share_rows, 1
    )
    local_latent = jnp.take(cache_latent, requests[0], axis=0, mode="clip")

    lengths_at = jnp.take(my_lengths, slot_at, mode="clip")

    def latents(piece):
        return lax.all_gather(piece, "tensor")

    if owners * depth == task_count:
        local = jnp.arange(depth, dtype=jnp.int32)
        attended = attend(
            slot_at[:depth],
            local,
            requests[0],
            lengths_at[:depth],
            queries,
            latents(local_latent),
            cache_values,
            key_up,
            own_latent,
            new_values,
            None,
        )
        gathered = {d: latents(in_flight[latent_at[d]]) for d in shifts}
        for (d, i), message in value_at.items():
            values = in_flight[message]
            size = values.shape[0]
            here = slice(d * depth + i * size, d * depth + (i + 1) * size)
            attended = attend(
                slot_at[here],
                local[i * size : (i + 1) * size],
                local[:size],
                lengths_at[here],
                queries,
                gathered[d],
                values,
                key_up,
                own_latent,
                new_values,
                attended,
            )
    else:
        pieces = [jnp.take(cache_values, requests[0], axis=0, mode="clip")]
        halves = [local_latent]
        for d in range(1, owners):
            halves.append(in_flight[latent_at[d]])
            pieces += [in_flight[m] for (e, _), m in value_at.items() if e == d]
        attended = attend(
            jnp.arange(task_count, dtype=jnp.int32),
            place,
            place,
            my_lengths,
            queries,
            latents(jnp.concatenate(halves)),
            jnp.concatenate(pieces),
            key_up,
            own_latent,
            new_values,
            None,
        )
    return attended, latent_out


def solution(mesh):
    return jax.shard_map(
        on_device,
        mesh=mesh,
        in_specs=(
            P(("groups", "dp"), None, "tensor"),
            P(("groups", "dp"), None, "tensor"),
            P(("groups", "dp"), None, "tensor"),
            P("tensor", None),
            P(None, "tensor"),
            P(("groups", "dp"), "tensor", None),
            P(("groups", "dp"), None, "tensor"),
            P("groups"),
            P("groups"),
        ),
        out_specs=(P(("groups", "dp"), None, "tensor"), P(("groups", "dp"), "tensor", None)),
        check_vma=False,
    )
```

```python
import functools
import math

import jax
import jax.numpy as jnp
from jax import lax
from jax.experimental import pallas as pl
from jax.experimental.pallas import tpu as pltpu
from jax.sharding import PartitionSpec as P

HD = 128
SCALE = HD ** (-0.5)
POWER = SCALE * math.log2(math.e)
LOW = -1e30


def attend_kernel(
    slot_ref,
    latent_place_ref,
    value_place_ref,
    length_ref,
    query_ref,
    latent_ref,
    value_ref,
    up_ref,
    own_latent_ref,
    own_value_ref,
    *rest,
):
    out_ref, rows_ref, keys_ref = rest[-3:]
    new_rows = query_ref.shape[1]
    per_kv = query_ref.shape[2] // HD
    parts, _, part_rows, _ = latent_ref.shape
    longest = parts * part_rows
    step = math.gcd(longest, 256)
    all_rows = per_kv * new_rows
    block = math.gcd(all_rows, 256)
    length = length_ref[pl.program_id(0)]
    up = up_ref[...]
    for g in range(per_kv):
        rows_ref[g * new_rows : (g + 1) * new_rows, :] = query_ref[0, :, g * HD : (g + 1) * HD]
    own_keys = jnp.dot(own_latent_ref[0], up, preferred_element_type=jnp.float32).astype(
        jnp.bfloat16
    )

    def attend(width):
        for p in range(width // part_rows):
            keys_ref[p * part_rows : (p + 1) * part_rows, :] = jnp.dot(
                latent_ref[p, 0], up, preferred_element_type=jnp.float32
            ).astype(jnp.bfloat16)
        for b in range(all_rows // block):
            rows = rows_ref[b * block : (b + 1) * block, :]
            scores = lax.dot_general(
                rows,
                keys_ref[0:width, :],
                (((1,), (1,)), ((), ())),
                preferred_element_type=jnp.float32,
            )
            first = width - step
            position = first + lax.broadcasted_iota(jnp.int32, (block, step), 1)
            last = jnp.where(position < length, scores[:, first:], LOW)
            scores = last if first == 0 else jnp.concatenate([scores[:, :first], last], axis=1)
            top_score = jnp.max(scores, axis=-1, keepdims=True)
            powers = jnp.exp2((scores - top_score) * POWER)
            total = jnp.sum(powers, axis=-1, keepdims=True)
            prefix = jnp.dot(
                powers.astype(jnp.bfloat16),
                value_ref[0, 0:width, :],
                preferred_element_type=jnp.float32,
            )
            prefix = (prefix / total).astype(jnp.bfloat16).astype(jnp.float32)
            log_total = top_score * SCALE + jnp.log(total)
            own = (
                lax.dot_general(
                    rows, own_keys, (((1,), (1,)), ((), ())), preferred_element_type=jnp.float32
                )
                * SCALE
            )
            row = lax.broadcasted_iota(jnp.int32, own.shape, 0) % new_rows
            own = jnp.where(row >= lax.broadcasted_iota(jnp.int32, own.shape, 1), own, LOW)
            own_max = jnp.max(own, axis=-1, keepdims=True)
            own_powers = jnp.exp(own - own_max)
            own_total = jnp.sum(own_powers, axis=-1, keepdims=True)
            own_sum = jnp.dot(
                own_powers.astype(jnp.bfloat16),
                own_value_ref[0],
                preferred_element_type=jnp.float32,
            )
            top = jnp.maximum(log_total, own_max)
            prefix_weight = jnp.exp(log_total - top)
            own_weight = jnp.exp(own_max - top)
            merged = (prefix_weight * prefix + own_weight * own_sum) / (
                prefix_weight + own_weight * own_total
            )
            merged = merged.astype(jnp.bfloat16)
            for i in range(block // new_rows):
                g = b * (block // new_rows) + i
                out_ref[0, :, g * HD : (g + 1) * HD] = merged[i * new_rows : (i + 1) * new_rows]

    for width in range(step, longest + 1, step):
        pl.when((length > width - step) & (length <= width))(functools.partial(attend, width))


def attend(
    slots,
    latent_places,
    value_places,
    lengths,
    queries,
    latents,
    values,
    key_up,
    own_latent,
    own_values,
    before,
):
    tasks = slots.shape[0]
    _, new_rows, qwidth = queries.shape
    parts, _, part_rows, rank = latents.shape
    longest, kwidth = values.shape[1:]
    kv_heads = kwidth // HD
    width = qwidth // kv_heads
    in_specs = [
        pl.BlockSpec((1, new_rows, width), lambda t, h, s, p, v, n: (s[t], 0, h)),
        pl.BlockSpec((parts, 1, part_rows, rank), lambda t, h, s, p, v, n: (0, p[t], 0, 0)),
        pl.BlockSpec((1, longest, HD), lambda t, h, s, p, v, n: (v[t], 0, h)),
        pl.BlockSpec((rank, HD), lambda t, h, s, p, v, n: (0, h)),
        pl.BlockSpec((1, new_rows, rank), lambda t, h, s, p, v, n: (s[t], 0, 0)),
        pl.BlockSpec((1, new_rows, HD), lambda t, h, s, p, v, n: (s[t], 0, h)),
    ]
    operands = [
        slots,
        latent_places,
        value_places,
        lengths,
        queries,
        latents,
        values,
        key_up,
        own_latent,
        own_values,
    ]
    aliases = {}
    if before is not None:
        in_specs.append(pl.BlockSpec(memory_space=pl.ANY))
        aliases = {len(operands): 0}
        operands.append(before)
    rows = width // HD * new_rows
    return pl.pallas_call(
        attend_kernel,
        grid_spec=pltpu.PrefetchScalarGridSpec(
            num_scalar_prefetch=4,
            grid=(tasks, kv_heads),
            in_specs=in_specs,
            out_specs=pl.BlockSpec((1, new_rows, width), lambda t, h, s, p, v, n: (s[t], 0, h)),
            scratch_shapes=[
                pltpu.VMEM((rows, HD), jnp.bfloat16),
                pltpu.VMEM((longest, HD), jnp.bfloat16),
            ],
        ),
        out_shape=jax.ShapeDtypeStruct(queries.shape, queries.dtype),
        input_output_aliases=aliases,
        compiler_params=pltpu.CompilerParams(vmem_limit_bytes=60 * 1024 * 1024),
        cost_estimate=pl.CostEstimate(
            flops=tasks * kv_heads * rows * longest * HD * 8,
            bytes_accessed=tasks * (2 * new_rows * qwidth + longest * (kwidth + rank)) * 2,
            transcendentals=tasks * kv_heads * rows * longest,
        ),
    )(*operands)


def on_device(
    queries,
    new_keys,
    new_values,
    key_down,
    key_up,
    cache_latent,
    cache_values,
    cache_lengths,
    task_source,
):
    task_count, new_rows, _ = queries.shape
    owners = lax.axis_size("dp")
    me = lax.axis_index("dp")
    depth = max(2, task_count // owners)
    share_rows = new_rows // lax.axis_size("tensor")

    source = task_source.reshape(owners, task_count)
    request = source % task_count
    distance = (owners - source[0] // task_count) % owners
    same = distance[:, None] == distance[None, :]
    earlier = jnp.arange(task_count)[None, :] < jnp.arange(task_count)[:, None]
    place = distance * depth + jnp.sum(same & earlier, axis=1)
    places = jnp.arange(owners * depth)
    slot_at = jnp.sum(
        jnp.where(place[None, :] == places[:, None], jnp.arange(task_count)[None, :], 0), axis=1
    ).astype(jnp.int32)
    my_source = lax.dynamic_index_in_dim(source, me, 0, keepdims=False)
    my_lengths = jnp.take(cache_lengths, my_source, mode="clip")

    def picked(shift):
        wanted = lax.dynamic_index_in_dim(request, (me + shift) % owners, 0, keepdims=False)
        return jnp.take(wanted, slot_at[shift * depth : (shift + 1) * depth], mode="clip")

    in_flight = []

    def send(array, shift, before=None):
        held = in_flight[-2:-1]
        array, held, before = lax.optimization_barrier((array, held, before))
        in_flight[-2:-1] = held
        pairs = [(i, (i + shift) % owners) for i in range(owners)]
        in_flight.append(lax.ppermute(array, "dp", pairs))
        return before

    def rows_of(array, which):
        return jnp.take(array, which, axis=0, mode="clip")

    shifts = sorted(range(1, owners), key=lambda d: (min(d, owners - d), d))
    requests = [picked(d) for d in range(owners)]
    for d in shifts:
        send(rows_of(cache_latent, requests[d]), d)

    all_keys = lax.all_gather(new_keys, "tensor")
    all_down = lax.all_gather(key_down, "tensor")
    own_latent = jnp.einsum(
        "trck,tkl->rcl", all_keys, all_down, preferred_element_type=jnp.float32
    ).astype(jnp.bfloat16)
    latent_out = lax.dynamic_slice_in_dim(
        own_latent, lax.axis_index("tensor") * share_rows, share_rows, 1
    )
    local_latent = rows_of(cache_latent, requests[0])
    lengths_at = jnp.take(my_lengths, slot_at, mode="clip")

    def latents(piece):
        return lax.all_gather(piece, "tensor")

    pieces = []
    for d in shifts:
        count = depth if d == shifts[-1] else 1
        pieces += [(d, i * depth // count, depth // count) for i in range(count)]
    first_value = len(shifts)

    if owners * depth == task_count:
        local = jnp.arange(depth, dtype=jnp.int32)

        def run(latent, values, value_places, start, offset, size, before):
            here = slice(start + offset, start + offset + size)
            return attend(
                slot_at[here],
                local[offset : offset + size],
                value_places,
                lengths_at[here],
                queries,
                latent,
                values,
                key_up,
                own_latent,
                new_values,
                before,
            )

        gathered = {}

        def run_piece(k, before):
            d, offset, size = pieces[k]
            if d not in gathered:
                gathered[d] = latents(in_flight[shifts.index(d)])
            values = in_flight[first_value + k]
            return run(gathered[d], values, local[:size], d * depth, offset, size, before)

        attended = run(latents(local_latent), cache_values, requests[0], 0, 0, depth, None)
        done = 0
        for k, (d, offset, size) in enumerate(pieces):
            if k > 2:
                attended = run_piece(done, attended)
                done += 1
            values = rows_of(cache_values, requests[d][offset : offset + size])
            if k >= 2:
                attended = send(values, d, attended)
            else:
                send(values, d)
        for k in range(done, len(pieces)):
            attended = run_piece(k, attended)
    else:
        for d in shifts:
            send(rows_of(cache_values, requests[d]), d)
        order = [shifts.index(d) for d in range(1, owners)]
        attended = attend(
            jnp.arange(task_count, dtype=jnp.int32),
            place,
            place,
            my_lengths,
            queries,
            latents(jnp.concatenate([local_latent] + [in_flight[i] for i in order])),
            jnp.concatenate(
                [rows_of(cache_values, requests[0])] + [in_flight[first_value + i] for i in order]
            ),
            key_up,
            own_latent,
            new_values,
            None,
        )
    return attended, latent_out


def solution(mesh):
    return jax.shard_map(
        on_device,
        mesh=mesh,
        in_specs=(
            P(("groups", "dp"), None, "tensor"),
            P(("groups", "dp"), None, "tensor"),
            P(("groups", "dp"), None, "tensor"),
            P("tensor", None),
            P(None, "tensor"),
            P(("groups", "dp"), "tensor", None),
            P(("groups", "dp"), None, "tensor"),
            P("groups"),
            P("groups"),
        ),
        out_specs=(P(("groups", "dp"), None, "tensor"), P(("groups", "dp"), "tensor", None)),
        check_vma=False,
    )
```

```python
import functools
import math

import jax
import jax.numpy as jnp
from jax import lax
from jax.experimental import pallas as pl
from jax.experimental.pallas import tpu as pltpu
from jax.sharding import PartitionSpec as P

HD = 128
SCALE = HD ** (-0.5)
POWER = SCALE * math.log2(math.e)
LOW = -1e30


def attend_kernel(
    slot_ref,
    latent_place_ref,
    value_place_ref,
    length_ref,
    query_ref,
    latent_ref,
    value_ref,
    up_ref,
    own_latent_ref,
    own_value_ref,
    *rest,
):
    out_ref, rows_ref, keys_ref = rest[-3:]
    new_rows = query_ref.shape[1]
    per_kv = query_ref.shape[2] // HD
    parts, _, part_rows, _ = latent_ref.shape
    longest = parts * part_rows
    step = math.gcd(longest, 256)
    all_rows = per_kv * new_rows
    block = all_rows // 2
    length = length_ref[pl.program_id(0)]
    up = up_ref[...]
    for g in range(per_kv):
        rows_ref[g * new_rows : (g + 1) * new_rows, :] = query_ref[0, :, g * HD : (g + 1) * HD]
    own_keys = jnp.dot(own_latent_ref[0], up, preferred_element_type=jnp.float32).astype(
        jnp.bfloat16
    )

    def attend(width):
        for p in range(width // part_rows):
            keys_ref[p * part_rows : (p + 1) * part_rows, :] = jnp.dot(
                latent_ref[p, 0], up, preferred_element_type=jnp.float32
            ).astype(jnp.bfloat16)
        blocks = range(all_rows // block)
        rows = [rows_ref[b * block : (b + 1) * block, :] for b in blocks]

        def scores_of(b):
            scores = lax.dot_general(
                rows[b],
                keys_ref[0:width, :],
                (((1,), (1,)), ((), ())),
                preferred_element_type=jnp.float32,
            )
            first = width - step
            position = first + lax.broadcasted_iota(jnp.int32, (block, step), 1)
            last = jnp.where(position < length, scores[:, first:], LOW)
            return last if first == 0 else jnp.concatenate([scores[:, :first], last], axis=1)

        def own_of(b):
            own = (
                lax.dot_general(
                    rows[b], own_keys, (((1,), (1,)), ((), ())), preferred_element_type=jnp.float32
                )
                * SCALE
            )
            shape = (block // new_rows, new_rows, new_rows)
            row = lax.broadcasted_iota(jnp.int32, shape, 1).reshape(block, new_rows)
            own = jnp.where(row >= lax.broadcasted_iota(jnp.int32, own.shape, 1), own, LOW)
            own_max = jnp.max(own, axis=-1, keepdims=True)
            own_powers = jnp.exp(own - own_max)
            own_total = jnp.sum(own_powers, axis=-1, keepdims=True)
            own_sum = jnp.dot(
                own_powers.astype(jnp.bfloat16),
                own_value_ref[0],
                preferred_element_type=jnp.float32,
            )
            return own_max, own_total, own_sum

        scores = [scores_of(b) for b in blocks]
        owned = [own_of(b) for b in blocks]
        tops = [jnp.max(scores[b], axis=-1, keepdims=True) for b in blocks]
        powers = [jnp.exp2((scores[b] - tops[b]) * POWER) for b in blocks]
        totals = [jnp.sum(powers[b], axis=-1, keepdims=True) for b in blocks]
        sums = [
            jnp.dot(
                powers[b].astype(jnp.bfloat16),
                value_ref[0, 0:width, :],
                preferred_element_type=jnp.float32,
            )
            for b in blocks
        ]
        for b in blocks:
            prefix = (sums[b] / totals[b]).astype(jnp.bfloat16).astype(jnp.float32)
            log_total = tops[b] * SCALE + jnp.log(totals[b])
            own_max, own_total, own_sum = owned[b]
            top = jnp.maximum(log_total, own_max)
            prefix_weight = jnp.exp(log_total - top)
            own_weight = jnp.exp(own_max - top)
            merged = (prefix_weight * prefix + own_weight * own_sum) / (
                prefix_weight + own_weight * own_total
            )
            merged = merged.astype(jnp.bfloat16)
            for i in range(block // new_rows):
                g = b * (block // new_rows) + i
                out_ref[0, :, g * HD : (g + 1) * HD] = merged[i * new_rows : (i + 1) * new_rows]

    for width in range(step, longest + 1, step):
        pl.when((length > width - step) & (length <= width))(functools.partial(attend, width))


def attend(
    slots,
    latent_places,
    value_places,
    lengths,
    queries,
    latents,
    values,
    key_up,
    own_latent,
    own_values,
    before,
):
    tasks = slots.shape[0]
    _, new_rows, qwidth = queries.shape
    parts, _, part_rows, rank = latents.shape
    longest, kwidth = values.shape[1:]
    kv_heads = kwidth // HD
    width = qwidth // kv_heads
    in_specs = [
        pl.BlockSpec((1, new_rows, width), lambda t, h, s, p, v, n: (s[t], 0, h)),
        pl.BlockSpec((parts, 1, part_rows, rank), lambda t, h, s, p, v, n: (0, p[t], 0, 0)),
        pl.BlockSpec((1, longest, HD), lambda t, h, s, p, v, n: (v[t], 0, h)),
        pl.BlockSpec((rank, HD), lambda t, h, s, p, v, n: (0, h)),
        pl.BlockSpec((1, new_rows, rank), lambda t, h, s, p, v, n: (s[t], 0, 0)),
        pl.BlockSpec((1, new_rows, HD), lambda t, h, s, p, v, n: (s[t], 0, h)),
    ]
    operands = [
        slots,
        latent_places,
        value_places,
        lengths,
        queries,
        latents,
        values,
        key_up,
        own_latent,
        own_values,
    ]
    aliases = {}
    if before is not None:
        in_specs.append(pl.BlockSpec(memory_space=pl.ANY))
        aliases = {len(operands): 0}
        operands.append(before)
    rows = width // HD * new_rows
    return pl.pallas_call(
        attend_kernel,
        grid_spec=pltpu.PrefetchScalarGridSpec(
            num_scalar_prefetch=4,
            grid=(tasks, kv_heads),
            in_specs=in_specs,
            out_specs=pl.BlockSpec((1, new_rows, width), lambda t, h, s, p, v, n: (s[t], 0, h)),
            scratch_shapes=[
                pltpu.VMEM((rows, HD), jnp.bfloat16),
                pltpu.VMEM((longest, HD), jnp.bfloat16),
            ],
        ),
        out_shape=jax.ShapeDtypeStruct(queries.shape, queries.dtype),
        input_output_aliases=aliases,
        compiler_params=pltpu.CompilerParams(vmem_limit_bytes=60 * 1024 * 1024),
        cost_estimate=pl.CostEstimate(
            flops=tasks * kv_heads * rows * longest * HD * 8,
            bytes_accessed=tasks * (2 * new_rows * qwidth + longest * (kwidth + rank)) * 2,
            transcendentals=tasks * kv_heads * rows * longest,
        ),
    )(*operands)


def on_device(
    queries,
    new_keys,
    new_values,
    key_down,
    key_up,
    cache_latent,
    cache_values,
    cache_lengths,
    task_source,
):
    task_count, new_rows, _ = queries.shape
    owners = lax.axis_size("dp")
    me = lax.axis_index("dp")
    depth = max(2, task_count // owners)
    share_rows = new_rows // lax.axis_size("tensor")

    source = task_source.reshape(owners, task_count)
    request = source % task_count
    distance = (owners - source[0] // task_count) % owners
    same = distance[:, None] == distance[None, :]
    earlier = jnp.arange(task_count)[None, :] < jnp.arange(task_count)[:, None]
    place = distance * depth + jnp.sum(same & earlier, axis=1)
    places = jnp.arange(owners * depth)
    slot_at = jnp.sum(
        jnp.where(place[None, :] == places[:, None], jnp.arange(task_count)[None, :], 0), axis=1
    ).astype(jnp.int32)
    my_source = lax.dynamic_index_in_dim(source, me, 0, keepdims=False)
    my_lengths = jnp.take(cache_lengths, my_source, mode="clip")

    def picked(shift):
        wanted = lax.dynamic_index_in_dim(request, (me + shift) % owners, 0, keepdims=False)
        return jnp.take(wanted, slot_at[shift * depth : (shift + 1) * depth], mode="clip")

    in_flight = []

    def send(array, shift, before=None):
        held = in_flight[-2:-1]
        array, held, before = lax.optimization_barrier((array, held, before))
        in_flight[-2:-1] = held
        pairs = [(i, (i + shift) % owners) for i in range(owners)]
        in_flight.append(lax.ppermute(array, "dp", pairs))
        return before

    def rows_of(array, which):
        return jnp.take(array, which, axis=0, mode="clip")

    shifts = sorted(range(1, owners), key=lambda d: (min(d, owners - d), d))
    requests = [picked(d) for d in range(owners)]
    all_keys = lax.all_gather(new_keys, "tensor")
    all_down = lax.all_gather(key_down, "tensor")
    own_latent = jnp.einsum(
        "trck,tkl->rcl", all_keys, all_down, preferred_element_type=jnp.float32
    ).astype(jnp.bfloat16)
    latent_out = lax.dynamic_slice_in_dim(
        own_latent, lax.axis_index("tensor") * share_rows, share_rows, 1
    )
    lengths_at = jnp.take(my_lengths, slot_at, mode="clip")

    def latents(piece):
        return lax.all_gather(piece, "tensor")

    pieces = []
    for d in shifts:
        count = depth if d == shifts[-1] else 1
        pieces += [(d, i * depth // count, depth // count) for i in range(count)]
    items = [("latent", d, 0, depth) for d in shifts]
    sends = [("value", *piece) for piece in pieces]
    items = items[:1] + sends[:1] + items[1:] + sends[1:]
    index_of = {item[:3]: i for i, item in enumerate(items)}

    def load(item):
        kind, d, offset, size = item
        array = cache_latent if kind == "latent" else cache_values
        return rows_of(array, requests[d][offset : offset + size])

    opening = load(items[0])
    requests[0], opening = lax.optimization_barrier((requests[0], opening))
    local_latent = rows_of(cache_latent, requests[0])
    send(opening, items[0][1])

    if owners * depth == task_count:
        local = jnp.arange(depth, dtype=jnp.int32)

        def run(latent, values, value_places, start, offset, size, before):
            here = slice(start + offset, start + offset + size)
            return attend(
                slot_at[here],
                local[offset : offset + size],
                value_places,
                lengths_at[here],
                queries,
                latent,
                values,
                key_up,
                own_latent,
                new_values,
                before,
            )

        gathered = {}

        def run_piece(k, before):
            d, offset, size = pieces[k]
            if d not in gathered:
                gathered[d] = latents(in_flight[index_of["latent", d, 0]])
            values = in_flight[index_of["value", d, offset]]
            return run(gathered[d], values, local[:size], d * depth, offset, size, before)

        attended = run(latents(local_latent), cache_values, requests[0], 0, 0, depth, None)
        done = sent = 0
        for item in items[1:]:
            if item[0] == "latent" or sent < 2:
                send(load(item), item[1])
            else:
                if sent > 2:
                    attended = run_piece(done, attended)
                    done += 1
                attended = send(load(item), item[1], attended)
            sent += item[0] == "value"
        for k in range(done, len(pieces)):
            attended = run_piece(k, attended)
    else:
        for item in items[1:]:
            send(load(item), item[1])
        distances = range(1, owners)
        values_of = [
            in_flight[index_of["value", d, offset]] for d, offset, _ in sorted(pieces)
        ]
        latents_of = [in_flight[index_of["latent", d, 0]] for d in distances]
        attended = attend(
            jnp.arange(task_count, dtype=jnp.int32),
            place,
            place,
            my_lengths,
            queries,
            latents(jnp.concatenate([local_latent] + latents_of)),
            jnp.concatenate([rows_of(cache_values, requests[0])] + values_of),
            key_up,
            own_latent,
            new_values,
            None,
        )
    return attended, latent_out


def solution(mesh):
    return jax.shard_map(
        on_device,
        mesh=mesh,
        in_specs=(
            P(("groups", "dp"), None, "tensor"),
            P(("groups", "dp"), None, "tensor"),
            P(("groups", "dp"), None, "tensor"),
            P("tensor", None),
            P(None, "tensor"),
            P(("groups", "dp"), "tensor", None),
            P(("groups", "dp"), None, "tensor"),
            P("groups"),
            P("groups"),
        ),
        out_specs=(P(("groups", "dp"), None, "tensor"), P(("groups", "dp"), "tensor", None)),
        check_vma=False,
    )
```
